128 devices in a mesh: owner: 32 (over z, y, core), rep: 4 (over x).
Axes of the slice: x: 4, y: 4, z: 4, core: 2. Of those that a mesh axis runs over, the one named last changes fastest.
Arguments:
- feat_codes: bfloat16 [65536, 768], P('owner'), may hold values from -1 to 1
- feat_scales: bfloat16 [65536], P('owner'), may hold values from 0.5 to 4
- hist_codes: bfloat16 [65536, 1024], P('owner'), may hold values from -1 to 1
- hist_scales: bfloat16 [65536], P('owner'), may hold values from 0.5 to 4
- batch_rows: int32 [32, 4, 512], P('owner'), may hold values from 0 to 2047, as said below
- send_rows: int32 [32, 4, 32, 32], P('owner', 'rep'), may hold values from 0 to 2047
- send_counts: int32 [32, 4, 32], P('owner', 'rep'), may hold values from 1 to 32, as said below
- block_ids: int32 [32, 4, 4, 8], P('owner', 'rep'), may hold values from 0 to 11
- block_counts: int32 [32, 4, 4], P('owner', 'rep'), may hold values from 1 to 8
- tiles: bfloat16 [32, 4, 4, 8, 128, 128], P('owner', 'rep'), may hold values from -0.1875 to 0.1875
- w_one: bfloat16 [1536, 1024], replicated, may hold values from -0.15625 to 0.15625
- w_two: bfloat16 [2048, 1024], replicated, may hold values from -0.125 to 0.125
- cotangent: bfloat16 [32, 4, 512, 1024], P('owner', 'rep'), may hold values from -0.0234375 to 0.0234375
Outputs:
- new_hist_codes: bfloat16 [65536, 1024], P('owner')
- new_hist_scales: bfloat16 [65536], P('owner')
- grad_one: float32 [1536, 1024], P('owner')
- grad_two: float32 [2048, 1024], P('owner')
The draws below stay inside these ranges and needn't reach their ends.
Inputs may be any that keep to these rules, and one draw needn't show every extreme that they name: `batch_rows`: for each owner the rep groups' lists together hold every row of its shard exactly once. `send_rows`: entries at or past the matching send_counts are ignored. `send_counts`: in every rep group some batch receives 32 live rows from every owner. `block_ids`: entries at or past the matching block_counts are ignored; blocks may repeat.
All inputs are finite; a program needn't handle non-finite values.
Results may differ from the reference program's by a relative error of at most 0.013.
Values may be sent and summed in bfloat16 or wider, within the bound.
A program may use at most 128 MiB of HBM per device.

```python
import math
import jax
import jax.numpy as jnp
from jax import lax

F = 768
H = 1024
B = 512
HMAX = 32
BLK = 128
KB = 8
QB = 4
NODE_DEV = 2048
NODES = 65536
NB_TAB = 12
ROWS = 65536
N_OWNER = 32
N_REP = 4


def draw_batch_rows(key, part):
    key = jax.random.fold_in(key, 11)
    owner_keys = jax.random.split(key, N_OWNER)
    orders = jax.vmap(lambda each_key: jax.random.permutation(each_key, N_REP * B))(owner_keys)
    return orders.reshape(N_OWNER, N_REP, B).astype(jnp.int32)


def draw_send_counts(key, part):
    key = jax.random.fold_in(key, 23)
    first_key, second_key, pick_key = jax.random.split(key, 3)
    shape_all = (N_OWNER, N_REP, N_OWNER)
    first_draw = jax.random.randint(first_key, shape_all, 1, HMAX + 1)
    second_draw = jax.random.randint(second_key, shape_all, 1, HMAX + 1)
    lighter = jnp.minimum(first_draw, second_draw)
    receiver = jax.random.randint(pick_key, (N_REP,), 0, N_OWNER)
    full_column = jnp.arange(N_OWNER)[None, None, :] == receiver[None, :, None]
    return jnp.where(full_column, HMAX, lighter).astype(jnp.int32)


def touch_ends(result, rng, low, top_value):
    longest = result.shape.index(max(result.shape))
    spots = []
    for shift in (0, 1):
        where = [jax.random.randint(jax.random.fold_in(rng, axis), (), 0, length) for axis, length in enumerate(result.shape)]
        where[longest] = (where[longest] + shift) % result.shape[longest]
        spots.append(tuple(where))
    return result.at[spots[0]].set(low).at[spots[1]].set(top_value)


def steps_of(key, dims, shards, low, top_value):
    loudness = 1.0
    for dim, shards_of in shards:
        steps = jax.random.uniform(jax.random.fold_in(jax.random.fold_in(key, 6), dim), (shards_of,), jnp.float32, low / len(shards), top_value / len(shards))
        loudness = loudness * jnp.repeat(jnp.exp(steps), dims[dim] // shards_of).reshape((-1,) + (1,) * (len(dims) - 1 - dim))
    return loudness


def scatter_about(key, dims, scale, reach, cuts=(), held_as=jnp.bfloat16):
    entries = scale * jax.random.normal(key, dims, jnp.float32)
    if cuts:
        entries = entries * steps_of(key, dims, cuts, -0.22, 0.18)
    return jnp.clip(entries, -reach, reach).astype(held_as)


def setup_inputs(seed: int = 0) -> dict:
    streams_of = jax.random.split(jax.random.key(seed), 14)
    return {
        "feat_codes": jnp.clip(jax.random.uniform(streams_of[0], (NODES, F), jnp.float32, -1.0, 1.0) * steps_of(streams_of[0], (NODES, F), ((0, 32),), -0.4, 0.0), -1.0, 1.0).astype(jnp.bfloat16),
        "feat_scales": jnp.clip(jnp.exp(math.log(4.0) - 2.0794415 * jax.random.uniform(streams_of[1], (NODES,), jnp.float32) ** steps_of(streams_of[1], (NODES,), ((0, 32),), -0.2, 0.2)), 0.5, 4.0).astype(jnp.bfloat16),
        "hist_codes": jnp.clip(jax.random.uniform(streams_of[2], (NODES, H), jnp.float32, -1.0, 1.0) * steps_of(streams_of[2], (NODES, H), ((0, 32),), -0.4, 0.0), -1.0, 1.0).astype(jnp.bfloat16),
        "hist_scales": jnp.clip(jnp.exp(math.log(4.0) - 2.0794415 * jax.random.uniform(streams_of[3], (NODES,), jnp.float32) ** steps_of(streams_of[3], (NODES,), ((0, 32),), -0.2, 0.2)), 0.5, 4.0).astype(jnp.bfloat16),
        "batch_rows": draw_batch_rows(jax.random.fold_in(streams_of[13], 71), 0),
        "send_rows": touch_ends(jax.random.randint(streams_of[5], (N_OWNER, N_REP, N_OWNER, HMAX), 0, NODE_DEV), jax.random.fold_in(streams_of[5], 1), 0, NODE_DEV - 1).astype(jnp.int32),
        "send_counts": draw_send_counts(jax.random.fold_in(streams_of[13], 71), 0),
        "block_ids": touch_ends(jax.random.randint(streams_of[7], (N_OWNER, N_REP, QB, KB), 0, NB_TAB), jax.random.fold_in(streams_of[7], 1), 0, NB_TAB - 1).astype(jnp.int32),
        "block_counts": touch_ends(jax.random.randint(streams_of[8], (N_OWNER, N_REP, QB), 1, KB + 1), jax.random.fold_in(streams_of[8], 1), 1, KB).astype(jnp.int32),
        "tiles": scatter_about(streams_of[9], (N_OWNER, N_REP, QB, KB, BLK, BLK), (KB * BLK) ** -0.5, 0.1875, ((0, 32), (1, 4))),
        "w_one": scatter_about(streams_of[10], (2 * F, H), (2 * F) ** -0.5, 0.15625),
        "w_two": scatter_about(streams_of[11], (2 * H, H), (2 * H) ** -0.5, 0.125),
        "cotangent": scatter_about(streams_of[12], (N_OWNER, N_REP, B, H), (1.0 / ROWS ** 0.5), 0.0234375, ((0, 32), (1, 4))),
    }


def rounded(value_in):
    return lax.optimization_barrier(value_in.astype(jnp.bfloat16))


def swish_slope(pre_value):
    sigmoid_val = jax.nn.sigmoid(pre_value)
    return sigmoid_val * (1.0 + pre_value * (1.0 - sigmoid_val))


def dequant(code_rows, scale_rows):
    return rounded(code_rows.astype(jnp.float32) * scale_rows.astype(jnp.float32)[..., None])


def fetch_halo(code_table, scale_table, send_list, send_count):
    picked = jax.vmap(lambda table_one, list_one: table_one[list_one])(code_table, send_list)
    picked_scales = jax.vmap(lambda table_one, list_one: table_one[list_one])(scale_table, send_list)
    live_slot = jnp.arange(HMAX)[None, :] < send_count[:, None]
    picked = jnp.where(live_slot[:, :, None], picked, jnp.zeros_like(picked))
    picked_scales = jnp.where(live_slot, picked_scales, jnp.zeros_like(picked_scales))
    return dequant(picked, picked_scales).reshape(N_OWNER * HMAX, code_table.shape[2])


def aggregate(table, block_list, block_count, tile_block):
    row_width = table.shape[1]
    blocks = table.reshape(NB_TAB, BLK, row_width)[block_list]
    keep_mask = jnp.arange(KB)[None, :] < block_count[:, None]
    weights = jnp.where(keep_mask[:, :, None, None], tile_block, jnp.zeros_like(tile_block))
    summed = jnp.einsum("qkij,qkjw->qiw", weights.astype(jnp.float32), blocks.astype(jnp.float32))
    return rounded(summed.reshape(QB * BLK, row_width)), weights


def reference(feat_codes, feat_scales, hist_codes, hist_scales, batch_rows, send_rows, send_counts, block_ids, block_counts, tiles, w_one, w_two, cotangent):
    feat_table = feat_codes.reshape(N_OWNER, NODE_DEV, F)
    feat_scale_table = feat_scales.reshape(N_OWNER, NODE_DEV)
    hist_table = hist_codes.reshape(N_OWNER, NODE_DEV, H)
    hist_scale_table = hist_scales.reshape(N_OWNER, NODE_DEV)

    def one_batch(totals, batch_index):
        owner_index = batch_index // N_REP
        rep_index = batch_index % N_REP
        batch_list = batch_rows[owner_index, rep_index]
        batch_feat = dequant(feat_table[owner_index][batch_list], feat_scale_table[owner_index][batch_list])
        send_list = send_rows[:, rep_index, owner_index]
        send_count = send_counts[:, rep_index, owner_index]
        halo_feat = fetch_halo(feat_table, feat_scale_table, send_list, send_count)
        halo_hist = fetch_halo(hist_table, hist_scale_table, send_list, send_count)
        block_list = block_ids[owner_index, rep_index]
        block_count = block_counts[owner_index, rep_index]
        tile_block = tiles[owner_index, rep_index]
        agg_one, weights = aggregate(jnp.concatenate([batch_feat, halo_feat], 0), block_list, block_count, tile_block)
        left_one = jnp.concatenate([batch_feat, agg_one], 1)
        pre_one = jnp.dot(left_one, w_one, preferred_element_type=jnp.float32)
        hidden = rounded(jax.nn.silu(pre_one))
        agg_two, unused_weights = aggregate(jnp.concatenate([hidden, halo_hist], 0), block_list, block_count, tile_block)
        left_two = jnp.concatenate([hidden, agg_two], 1)
        pre_two = jnp.dot(left_two, w_two, preferred_element_type=jnp.float32)
        delta_two = rounded(cotangent[owner_index, rep_index].astype(jnp.float32) * swish_slope(pre_two))
        back_agg = rounded(jnp.dot(delta_two, w_two[H:].T, preferred_element_type=jnp.float32))
        direct_term = jnp.dot(delta_two, w_two[:H].T, preferred_element_type=jnp.float32)
        spread = jnp.einsum("qkij,qiw->qkjw", weights.astype(jnp.float32), back_agg.reshape(QB, BLK, H).astype(jnp.float32))
        table_grad = jnp.zeros((NB_TAB, BLK, H), jnp.float32).at[block_list.reshape(-1)].add(spread.reshape(QB * KB, BLK, H))
        delta_hidden = direct_term + table_grad[:QB].reshape(B, H)
        delta_one = rounded(delta_hidden * swish_slope(pre_one))
        term_one = jnp.dot(left_one.T, delta_one, preferred_element_type=jnp.float32)
        term_two = jnp.dot(left_two.T, delta_two, preferred_element_type=jnp.float32)
        magnitude = jnp.max(jnp.abs(hidden.astype(jnp.float32)), axis=1) + 1e-5
        new_scales = rounded(magnitude)
        new_codes = rounded(hidden.astype(jnp.float32) / new_scales.astype(jnp.float32)[:, None])
        return (totals[0] + term_one, totals[1] + term_two), (new_codes, new_scales)

    start_sums = (jnp.zeros((2 * F, H), jnp.float32), jnp.zeros((2 * H, H), jnp.float32))
    (grad_one, grad_two), (all_codes, all_scales) = lax.scan(one_batch, start_sums, jnp.arange(N_OWNER * N_REP, dtype=jnp.int32))
    placed = batch_rows.reshape(N_OWNER, NODE_DEV)
    new_hist_codes = jax.vmap(lambda place_rows, values: jnp.zeros_like(values).at[place_rows].set(values))(placed, all_codes.reshape(N_OWNER, NODE_DEV, H))
    new_hist_scales = jax.vmap(lambda place_rows, values: jnp.zeros_like(values).at[place_rows].set(values))(placed, all_scales.reshape(N_OWNER, NODE_DEV))
    return new_hist_codes.reshape(NODES, H), new_hist_scales.reshape(NODES), grad_one, grad_two
```

```python
import functools

import jax
import jax.numpy as jnp
from jax import lax
from jax.experimental import pallas as pl
from jax.experimental.pallas import tpu as pltpu
from jax.sharding import PartitionSpec as P

F = 768
H = 1024
B = 512
BLK = 128
KB = 8
QB = 4
NODE = 2048
NTAB = 12
MESH = pl.DeviceIdType.MESH
BF = jnp.bfloat16
F32 = jnp.float32

ROUNDS = (
    ((1, 0), (3, 0), (0, 1), (0, 3)),
    ((1, 1), (3, 3), (1, 3), (3, 1)),
    ((2, 0), (0, 2), (2, 2), (0, 0)),
    ((2, 1), (1, 2), (2, 3), (3, 2)),
)
PEERS = [(dz, dy, dc) for chips in ROUNDS for dc in (0, 1) for dz, dy in chips if (dz, dy, dc) != (0, 0, 0)]


def swish_slope(pre, sig):
    return sig * (1.0 + pre * (1.0 - sig))


def dot(left, right):
    return jnp.dot(left, right, preferred_element_type=F32)


def dot_rows(left, right):
    return lax.dot_general(left, right, (((0,), (0,)), ((), ())), preferred_element_type=F32)


def dot_cols(left, right):
    return lax.dot_general(left, right, (((1,), (1,)), ((), ())), preferred_element_type=F32)


def kernel(
    ids, brow, scales, idx_h, feat_h, hist_h, tiles_h, w1_h, w2_h, cot_h,
    hist_o, sc_o, g1_o, g2_o,
    table, w1, w2, tiles, cot, idxc, adj, sel, sendf, sendh, recvf, recvh,
    left1, left2, pre1, pre2, tmp, d2, back, d1, codes, scmsg, stage,
    part, r2, r1, pa, pb, pc, qa, qb, qc, pa2, pb2, pc2, qa2, qb2, qc2, pa3, pb3, pc3, gath,
    lsem, osem, fss, frs, hss, hrs, ass, ars, css, crs, rss, rrs,
):
    own = lax.axis_index("owner")
    x = lax.axis_index("rep")
    z = lax.div(own, 8)
    y = lax.rem(lax.div(own, 2), 4)
    c = lax.rem(own, 2)

    def at(dz, dy, dc, dx=0):
        zz, yy = lax.rem(z + dz, 4), lax.rem(y + dy, 4)
        return (zz * 8 + yy * 2 + lax.rem(c + dc, 2), lax.rem(x + dx, 4))

    def load(k, src, dst):
        cp = pltpu.make_async_copy(src, dst, lsem.at[k])
        cp.start()
        return cp

    def send(src, dst, ss, rs, k, dev):
        cp = pltpu.make_async_remote_copy(
            src_ref=src, dst_ref=dst, send_sem=ss.at[k], recv_sem=rs.at[k],
            device_id=dev, device_id_type=MESH,
        )
        cp.start()
        return cp

    ld_idx = load(0, idx_h, idxc)
    ld_feat = load(1, feat_h, table.at[:, pl.ds(0, F)])
    ld_tiles = load(2, tiles_h, tiles)
    ld_w1 = load(3, w1_h, w1)
    ld_w2 = load(4, w2_h, w2)
    ld_cot = load(5, cot_h, cot)

    bar = pltpu.get_barrier_semaphore()
    for dz, dy, dc in PEERS:
        pl.semaphore_signal(bar, inc=1, device_id=at(dz, dy, dc), device_id_type=MESH)
    for dx in (1, 2, 3):
        pl.semaphore_signal(bar, inc=1, device_id=at(0, 0, 0, dx), device_id_type=MESH)

    lane = lax.broadcasted_iota(jnp.int32, (64, 128), 1)

    def pick(starts, which):
        for i, start in enumerate(starts):
            col = idxc[pl.ds(pl.multiple_of(start, 64), 64), :]
            for t in range(NODE // 128):
                hit = col == lane + t * 128
                val = jnp.where(hit, scales[which : which + 1, t * 128 : (t + 1) * 128], 0.0)
                sel[i * 64 : (i + 1) * 64, t * 128 : (t + 1) * 128] = val.astype(BF)

    def halo(width, which, sendb, recvb, ss, rs, first):
        cps = []
        for chips in ROUNDS:
            nums = [lax.rem(z + dz, 4) * 4 + lax.rem(y + dy, 4) for dz, dy in chips]
            pick([n * 64 for n in nums], which)
            for t in range(width // 256):
                cols = slice(t * 256, (t + 1) * 256)
                res = dot(sel[...], table[:, cols]).astype(BF)
                for i, n in enumerate(nums):
                    sendb[n, :, cols] = res[i * 64 : (i + 1) * 64]
            if first:
                pl.semaphore_wait(bar, len(PEERS) + 3)
                first = False
            for dc in (0, 1):
                for n, (dz, dy) in zip(nums, chips):
                    cc = lax.rem(c + dc, 2)
                    src = sendb.at[n, pl.ds(pl.multiple_of(cc * 32, 32), 32)]
                    mine = pl.ds(pl.multiple_of(own * 32, 32), 32)
                    if (dz, dy, dc) == (0, 0, 0):
                        recvb[mine, :] = src[...]
                    else:
                        cps.append(send(src, recvb.at[mine], ss, rs, len(cps), at(dz, dy, dc)))
        return cps

    ld_idx.wait()
    ld_feat.wait()
    cps_f = halo(F, 0, sendf, recvf, fss, frs, True)
    for i in range(2):
        pick([1024 + x * B + i * 256 + j * 64 for j in range(4)], 0)
        for t in range(F // 256):
            cols = slice(t * 256, (t + 1) * 256)
            left1[i * 256 : (i + 1) * 256, cols] = dot(sel[...], table[:, cols]).astype(BF)
    ld_hist = load(6, hist_h, table)

    ld_tiles.wait()

    def fill(q, carry):
        rows = pl.ds(pl.multiple_of(q * BLK, BLK), BLK)
        for b in range(NTAB):
            acc = jnp.zeros((BLK, BLK), F32)
            for k in range(KB):
                acc += jnp.where(ids[q * KB + k] == b, tiles[q, k], jnp.zeros((), BF)).astype(F32)
            adj[rows, b * BLK : (b + 1) * BLK] = acc.astype(BF)
        return carry

    lax.fori_loop(0, QB, fill, 0)
    ld_hist.wait()
    cps_h = halo(H, 1, sendh, recvh, hss, hrs, False)

    ld_w1.wait()
    for i in range(2):
        rows = slice(i * 256, (i + 1) * 256)
        tmp[rows, :F] = dot(adj[rows, :B], left1[:, :F])
        pre1[rows, :] = dot(left1[rows, :F], w1[:F, :])
    for cp in cps_f:
        cp.wait_recv()
    ag = []
    for i in range(2):
        rows = slice(i * 256, (i + 1) * 256)
        left1[rows, F:] = (tmp[rows, :F] + dot(adj[rows, B:], recvf[...])).astype(BF)
        pre = pre1[rows, :] + dot(left1[rows, F:], w1[F:, :])
        sig = jax.nn.sigmoid(pre)
        hid = (pre * sig).astype(BF)
        pre1[rows, :] = swish_slope(pre, sig)
        left2[rows, :H] = hid
        wide = hid.astype(F32)
        scale = (jnp.max(jnp.abs(wide), axis=1, keepdims=True) + 1e-5).astype(BF).astype(F32)
        mine = pl.ds(pl.multiple_of(x * B + i * 256, 256), 256)
        codes[mine, :] = (wide * (1.0 / scale)).astype(BF)
        for j in range(2):
            turned = jnp.broadcast_to(scale[j * 128 : (j + 1) * 128], (128, 128)).T
            scmsg[x, 2 * i + j : 2 * i + j + 1, :] = turned[0:1]
        ag.append(send(codes.at[mine], codes.at[mine], ass, ars, 2 * i, at(0, 0, 0, 1)))
        ag.append(send(codes.at[mine], codes.at[mine], ass, ars, 2 * i + 1, at(0, 0, 0, 3)))
    for dx in (1, 2, 3):
        ag.append(send(scmsg.at[x], scmsg.at[x], ass, ars, 5 + dx, at(0, 0, 0, dx)))

    ld_w2.wait()
    ld_cot.wait()
    for i in range(2):
        rows = slice(i * 256, (i + 1) * 256)
        tmp[rows, :] = dot(adj[rows, :B], left2[:, :H])
        pre2[rows, :] = dot(left2[rows, :H], w2[:H, :])

    ag[0].wait_recv()
    far = pl.ds(pl.multiple_of(lax.rem(x + 3, 4) * B, B), 256)
    fwd = [send(codes.at[far], codes.at[far], ass, ars, 4, at(0, 0, 0, 1))]
    ag[3].wait_recv()
    far = pl.ds(pl.multiple_of(lax.rem(x + 1, 4) * B + 256, 256), 256)
    fwd.append(send(codes.at[far], codes.at[far], ass, ars, 5, at(0, 0, 0, 3)))

    for cp in cps_h:
        cp.wait_recv()
    for i in range(2):
        rows = slice(i * 256, (i + 1) * 256)
        left2[rows, H:] = (tmp[rows, :] + dot(adj[rows, B:], recvh[...])).astype(BF)
        pre = pre2[rows, :] + dot(left2[rows, H:], w2[H:, :])
        sig = jax.nn.sigmoid(pre)
        d2[rows, :] = (cot[rows, :].astype(F32) * swish_slope(pre, sig)).astype(BF)

    def term(left, delta, share, recv, base):
        width = 8 * share

        def one(zt, carry):
            cols = pl.ds(pl.multiple_of(zt * width, 128), width)
            lhs = left[:, cols]
            for t in range(4):
                res = dot_rows(lhs, delta[:, t * 256 : (t + 1) * 256]).astype(BF)
                for o in range(8):
                    part[zt, o // 2, o % 2, t, :share, :] = res[o * share : (o + 1) * share]
            pltpu.make_async_remote_copy(
                src_ref=part.at[zt, :, 1 - c, :, pl.ds(0, share)], dst_ref=recv.at[zt],
                send_sem=css.at[base + zt], recv_sem=crs.at[base + zt],
                device_id=at(0, 0, 1), device_id_type=MESH,
            ).start()
            return carry

        lax.fori_loop(0, 4, one, 0)

    def merge(share, recv, base):
        def one(zt, carry):
            cp = pltpu.make_async_remote_copy(
                src_ref=part.at[zt, :, 1 - c, :, pl.ds(0, share)], dst_ref=recv.at[zt],
                send_sem=css.at[base + zt], recv_sem=crs.at[base + zt],
                device_id=at(0, 0, 1), device_id_type=MESH,
            )
            cp.wait()
            for t in range(4):
                both = recv[zt, t].astype(F32) + part[zt, t, c, :, :share, :].astype(F32)
                recv[zt, t] = both.astype(BF)
            return carry

        lax.fori_loop(0, 4, one, 0)

    def others(k):
        return [(i, lax.rem(k + i + 1, 4)) for i in range(3)]

    def first_phase(recv, s, base, offs):
        (a0, an), (b0, bn), (c0, cn) = s
        oa, ob, oc = offs
        cps = []
        for i in range(3):
            yy, zz, xx = (lax.rem(k + i + 1, 4) for k in (y, z, x))
            cps.append(send(recv.at[:, yy, :, pl.ds(a0, an)], pa.at[i, :, :, pl.ds(oa, an)], rss, rrs, base + i, at(0, i + 1, 0)))
            cps.append(send(recv.at[zz, :, :, pl.ds(b0, bn)], pb.at[i, :, :, pl.ds(ob, bn)], rss, rrs, base + 3 + i, at(i + 1, 0, 0)))
            cps.append(send(recv.at[:, :, xx, pl.ds(c0, cn)], pc.at[i, :, :, pl.ds(oc, cn)], rss, rrs, base + 6 + i, at(0, 0, 0, i + 1)))
        return cps

    term(left2, d2, 64, r2, 0)
    for i in range(2):
        rows = slice(i * 256, (i + 1) * 256)
        back[rows, :] = dot_cols(d2[rows, :], w2[H:, :]).astype(BF)
    for i in range(2):
        rows = slice(i * 256, (i + 1) * 256)
        grad = dot_cols(d2[rows, :], w2[:H, :]) + dot_rows(adj[:, rows], back[...])
        d1[rows, :] = (grad * pre1[rows, :]).astype(BF)
    merge(64, r2, 0)
    p1 = first_phase(r2, ((0, 32), (32, 16), (48, 16)), 0, (0, 0, 0))
    term(left1, d1, 48, r1, 4)
    merge(48, r1, 4)
    p1 += first_phase(r1, ((0, 16), (16, 16), (32, 16)), 9, (32, 16, 16))

    for cp in [ag[1], ag[2]] + ag[4:] + fwd:
        cp.wait_recv()
    sub = lax.broadcasted_iota(jnp.int32, (256, 256), 0)

    def place(n, carry):
        for t in range(NODE // 256):
            cols = slice(t * 256, (t + 1) * 256)
            hit = sub + n * 256 == brow[0:1, cols]
            sel[:, cols] = jnp.where(hit, 1.0, 0.0).astype(BF)
        slot = lax.rem(n, 2)
        out = pltpu.make_async_copy(
            stage.at[slot], hist_o.at[pl.ds(pl.multiple_of(n * 256, 256), 256)], osem.at[slot]
        )

        @pl.when(n >= 2)
        def _():
            out.wait()

        for t in range(4):
            cols = slice(t * 256, (t + 1) * 256)
            stage[slot, :, cols] = dot(sel[...], codes[:, cols]).astype(BF)
        out.start()
        return carry

    lax.fori_loop(0, 8, place, 0)
    for slot in range(2):
        pltpu.make_async_copy(stage.at[slot], hist_o.at[pl.ds(0, 256)], osem.at[slot]).wait()

    sc_o[...] = jnp.zeros((8, NODE), F32)
    lane_w = lax.broadcasted_iota(jnp.int32, (128, 128), 1)

    def place_scale(k, carry):
        rr, j = lax.div(k, 4), lax.rem(k, 4)
        col = idxc[pl.ds(pl.multiple_of(1024 + k * 128, 128), 128), :]
        val = jnp.broadcast_to(scmsg[rr, pl.ds(j, 1), :], (128, 128)).T
        for t in range(NODE // 128):
            got = jnp.where(col == lane_w + t * 128, val, 0.0)
            sc_o[:, t * 128 : (t + 1) * 128] += jnp.sum(got.reshape(16, 8, 128), axis=0)
        return carry

    lax.fori_loop(0, 16, place_scale, 0)

    def wait(cps):
        for cp in cps:
            cp.wait_recv()

    def total(mine, got, *at_index):
        acc = mine.astype(F32)
        for i in range(3):
            acc += got[(i, *at_index)].astype(F32)
        return acc.astype(BF)

    wait(p1)

    def sum_one(k, carry):
        qa[k, :, 0:32] = total(r2[k, y, :, 0:32], pa, k, slice(None), slice(0, 32))
        qa[k, :, 32:48] = total(r1[k, y, :, 0:16], pa, k, slice(None), slice(32, 48))
        qb[k, :, 0:16] = total(r2[z, k, :, 32:48], pb, k, slice(None), slice(0, 16))
        qb[k, :, 16:32] = total(r1[z, k, :, 16:32], pb, k, slice(None), slice(16, 32))
        qc[k, :, 0:16] = total(r2[k, :, x, 48:64], pc, k, slice(None), slice(0, 16))
        qc[k, :, 16:32] = total(r1[k, :, x, 32:48], pc, k, slice(None), slice(16, 32))
        return carry

    lax.fori_loop(0, 4, sum_one, 0)
    p2 = []
    for i in range(3):
        yy, zz = lax.rem(y + i + 1, 4), lax.rem(z + i + 1, 4)
        p2.append(send(qa.at[zz], pa2.at[i], rss, rrs, 18 + i, at(i + 1, 0, 0)))
        p2.append(send(qb.at[yy], pb2.at[i], rss, rrs, 21 + i, at(0, i + 1, 0)))
        p2.append(send(qc.at[:, yy], pc2.at[i], rss, rrs, 24 + i, at(0, i + 1, 0)))
    wait(p2)

    def sum_two(k, carry):
        qa2[k] = total(qa[z, k], pa2, k)
        qb2[k] = total(qb[y, k], pb2, k)
        qc2[k] = total(qc[k, y], pc2, k)
        return carry

    lax.fori_loop(0, 4, sum_two, 0)
    p3 = []
    for i in range(3):
        xx, zz = lax.rem(x + i + 1, 4), lax.rem(z + i + 1, 4)
        p3.append(send(qa2.at[xx], pa3.at[i], rss, rrs, 27 + i, at(0, 0, 0, i + 1)))
        p3.append(send(qb2.at[xx], pb3.at[i], rss, rrs, 30 + i, at(0, 0, 0, i + 1)))
        p3.append(send(qc2.at[zz], pc3.at[i], rss, rrs, 33 + i, at(i + 1, 0, 0)))
    wait(p3)
    gath[x, 0:48] = total(qa2[x], pa3)
    gath[x, 48:80] = total(qb2[x], pb3)
    gath[x, 80:112] = total(qc2[z], pc3)
    p4 = [send(gath.at[x], gath.at[x], rss, rrs, 36 + i, at(0, 0, 0, i + 1)) for i in range(3)]
    wait(p4)
    for t in range(4):
        cols = slice(t * 256, (t + 1) * 256)
        got = gath[t].astype(F32)
        g2_o[0:32, cols] = got[0:32]
        g1_o[0:16, cols] = got[32:48]
        g2_o[32:48, cols] = got[48:64]
        g1_o[16:32, cols] = got[64:80]
        g2_o[48:64, cols] = got[80:96]
        g1_o[32:48, cols] = got[96:112]
    for cp in cps_f + cps_h + ag + fwd + p1 + p2 + p3 + p4:
        cp.wait_send()


def shards(feat_codes, feat_scales, hist_codes, hist_scales, batch_rows, send_rows, send_counts,
           block_ids, block_counts, tiles, w_one, w_two, cotangent):
    live = jnp.arange(32)[None, :] < send_counts[0, 0][:, None]
    picks = jnp.where(live, send_rows[0, 0], -1).reshape(-1)
    placed = batch_rows[0].reshape(-1)
    idx = jnp.broadcast_to(jnp.concatenate([picks, placed])[:, None], (3072, 128))
    ids = jnp.where(jnp.arange(KB)[None, :] < block_counts[0, 0][:, None], block_ids[0, 0], -1).reshape(-1)
    scales = jnp.stack([feat_scales, hist_scales]).astype(F32)
    hbm = pl.BlockSpec(memory_space=pl.ANY)
    vmem = pl.BlockSpec(memory_space=pltpu.VMEM)
    smem = pl.BlockSpec(memory_space=pltpu.SMEM)
    v = pltpu.VMEM
    dma = pltpu.SemaphoreType.DMA
    scratch = [
        v((NODE, H), BF), v((2 * F, H), BF), v((2 * H, H), BF), v((QB, KB, BLK, BLK), BF), v((B, H), BF),
        v((3072, 128), jnp.int32), v((B, NTAB * BLK), BF), v((256, NODE), BF),
        v((16, 64, F), BF), v((16, 64, H), BF), v((1024, F), BF), v((1024, H), BF),
        v((B, 2 * F), BF), v((B, 2 * H), BF), v((B, H), F32), v((B, H), F32), v((B, H), F32),
        v((B, H), BF), v((B, H), BF), v((B, H), BF), v((4 * B, H), BF), v((4, 8, 128), F32),
        v((2, 256, H), BF),
        v((4, 4, 2, 4, 64, 256), BF), v((4, 4, 4, 64, 256), BF), v((4, 4, 4, 48, 256), BF),
        v((3, 4, 4, 48, 256), BF), v((3, 4, 4, 32, 256), BF), v((3, 4, 4, 32, 256), BF),
        v((4, 4, 48, 256), BF), v((4, 4, 32, 256), BF), v((4, 4, 32, 256), BF),
        v((3, 4, 48, 256), BF), v((3, 4, 32, 256), BF), v((3, 4, 32, 256), BF),
        v((4, 48, 256), BF), v((4, 32, 256), BF), v((4, 32, 256), BF),
        v((3, 48, 256), BF), v((3, 32, 256), BF), v((3, 32, 256), BF),
        v((4, 112, 256), BF),
        dma((7,)), dma((2,)), dma((31,)), dma((31,)), dma((31,)), dma((31,)),
        dma((9,)), dma((9,)), dma((8,)), dma((8,)), dma((39,)), dma((39,)),
    ]
    hist_out, sc, g1, g2 = pl.pallas_call(
        kernel,
        out_shape=(
            jax.ShapeDtypeStruct((NODE, H), BF),
            jax.ShapeDtypeStruct((8, NODE), F32),
            jax.ShapeDtypeStruct((48, H), F32),
            jax.ShapeDtypeStruct((64, H), F32),
        ),
        in_specs=[smem, vmem, vmem] + [hbm] * 7,
        out_specs=(hbm, vmem, vmem, vmem),
        scratch_shapes=scratch,
        compiler_params=pltpu.CompilerParams(
            collective_id=0, has_side_effects=True, vmem_limit_bytes=62 << 20
        ),
        cost_estimate=pl.CostEstimate(flops=30_000_000_000, bytes_accessed=30_000_000, transcendentals=1_000_000),
    )(
        ids, placed[None, :], scales, idx, feat_codes, hist_codes, tiles[0, 0], w_one, w_two, cotangent[0, 0]
    )
    return hist_out, jnp.sum(sc, axis=0).astype(BF), g1, g2


def solution(mesh):
    in_specs = (
        P("owner", None), P("owner"), P("owner", None), P("owner"), P("owner", None, None),
        P("owner", "rep", None, None), P("owner", "rep", None), P("owner", "rep", None, None),
        P("owner", "rep", None), P("owner", "rep", None, None, None, None), P(), P(),
        P("owner", "rep", None, None),
    )
    out_specs = (P("owner", None), P("owner"), P("owner", None), P("owner", None))
    return jax.shard_map(shards, mesh=mesh, in_specs=in_specs, out_specs=out_specs, check_vma=False)
```

```python
import functools

import jax
import jax.numpy as jnp
from jax import lax
from jax.experimental import pallas as pl
from jax.experimental.pallas import tpu as pltpu
from jax.sharding import PartitionSpec as P

F = 768
H = 1024
B = 512
BLK = 128
KB = 8
QB = 4
NODE = 2048
NTAB = 12
MESH = pl.DeviceIdType.MESH
BF = jnp.bfloat16
F32 = jnp.float32

ROUNDS = (
    ((1, 0), (3, 0), (0, 1), (0, 3)),
    ((1, 1), (3, 3), (1, 3), (3, 1)),
    ((2, 0), (0, 2), (2, 2), (0, 0)),
    ((2, 1), (1, 2), (2, 3), (3, 2)),
)
PEERS = [(dz, dy, dc) for chips in ROUNDS for dc in (0, 1) for dz, dy in chips if (dz, dy, dc) != (0, 0, 0)]


def swish_slope(pre, sig):
    return sig * (1.0 + pre * (1.0 - sig))


def dot(left, right):
    return jnp.dot(left, right, preferred_element_type=F32)


def dot_rows(left, right):
    return lax.dot_general(left, right, (((0,), (0,)), ((), ())), preferred_element_type=F32)


def dot_cols(left, right):
    return lax.dot_general(left, right, (((1,), (1,)), ((), ())), preferred_element_type=F32)


def kernel(
    ids, counts, brow_h, srow_h, scount_h, fscale_h, hscale_h, feat_h, hist_h, tiles_h, w1_h, w2_h, cot_h,
    hist_o, sc_o, two_o, one_o,
    brow, srow, scount, fscale, hscale, sc,
    table, w1, w2, tiles, cot, idxc, adj, adjt, sel, sendf, sendh, recvf, recvh,
    left1, left2, pre1, pre2, tmp, d2, d1, codes, scmsg, stage, part,
    r2, pa2, pb2, pc2, qa2, qb2, qc2, ra2, rb2, rc2, g2,
    r1, pa1, pb1, pc1, qa1, qb1, qc1, ra1, rb1, rc1, g1,
    lsem, osem, fss, frs, hss, hrs, ass, ars, css, crs, rss, rrs,
):
    own = lax.axis_index("owner")
    x = lax.axis_index("rep")
    z = lax.div(own, 8)
    y = lax.rem(lax.div(own, 2), 4)
    c = lax.rem(own, 2)

    def at(dz, dy, dc, dx=0):
        zz, yy = lax.rem(z + dz, 4), lax.rem(y + dy, 4)
        return (zz * 8 + yy * 2 + lax.rem(c + dc, 2), lax.rem(x + dx, 4))

    def load(k, src, dst):
        cp = pltpu.make_async_copy(src, dst, lsem.at[k])
        cp.start()
        return cp

    def send(src, dst, ss, rs, k, dev):
        cp = pltpu.make_async_remote_copy(
            src_ref=src, dst_ref=dst, send_sem=ss.at[k], recv_sem=rs.at[k],
            device_id=dev, device_id_type=MESH,
        )
        cp.start()
        return cp

    bar = pltpu.get_barrier_semaphore()
    for dz, dy, dc in PEERS:
        pl.semaphore_signal(bar, inc=1, device_id=at(dz, dy, dc), device_id_type=MESH)
    for dx in (1, 2, 3):
        pl.semaphore_signal(bar, inc=1, device_id=at(0, 0, 0, dx), device_id_type=MESH)

    smalls = [
        load(7 + i, src, dst)
        for i, (src, dst) in enumerate(
            ((scount_h, scount), (srow_h, srow), (brow_h, brow), (fscale_h, fscale), (hscale_h, hscale))
        )
    ]
    ld_feat = load(1, feat_h, table.at[:, pl.ds(0, F)])
    ld_tiles = load(2, tiles_h, tiles)
    ld_w1 = load(3, w1_h, w1)
    ld_w2 = load(4, w2_h, w2)
    ld_cot = load(5, cot_h, cot)
    for cp in smalls:
        cp.wait()

    alive = lax.broadcasted_iota(jnp.int32, (32, 32), 0) < scount[0]
    turned = jnp.where(alive, srow[0, 0].T, -1)
    for d in range(32):
        idxc[d * 32 : (d + 1) * 32, :] = jnp.broadcast_to(turned[:, d : d + 1], (32, 128))

    def spread(k, carry):
        line = brow[0, pl.ds(k, 1), :]
        for j in range(4):
            wide = jnp.broadcast_to(line[:, j * 128 : (j + 1) * 128], (128, 128)).T
            idxc[pl.ds(pl.multiple_of(1024 + k * B + j * 128, 128), 128), :] = wide
        return carry

    lax.fori_loop(0, 4, spread, 0)
    scales = (fscale[...].astype(F32).reshape(1, NODE), hscale[...].astype(F32).reshape(1, NODE))

    lane = lax.broadcasted_iota(jnp.int32, (64, 128), 1)

    def pick(starts, which):
        for i, start in enumerate(starts):
            col = idxc[pl.ds(pl.multiple_of(start, 64), 64), :]
            for t in range(NODE // 128):
                hit = col == lane + t * 128
                val = jnp.where(hit, scales[which][:, t * 128 : (t + 1) * 128], 0.0)
                sel[i * 64 : (i + 1) * 64, t * 128 : (t + 1) * 128] = val.astype(BF)

    def halo(chips, width, which, sendb, recvb, ss, rs, first, gate):
        cps = []
        nums = [lax.rem(z + dz, 4) * 4 + lax.rem(y + dy, 4) for dz, dy in chips]
        pick([n * 64 for n in nums], which)
        for t in range(width // 256):
            cols = slice(t * 256, (t + 1) * 256)
            res = dot(sel[...], table[:, cols]).astype(BF)
            for i, n in enumerate(nums):
                sendb[n, :, cols] = res[i * 64 : (i + 1) * 64]
        if first == 0 and width == F:
            pl.semaphore_wait(bar, len(PEERS) + 3)
        for cp in gate:
            cp.wait_send()
        for dc in (0, 1):
            for n, (dz, dy) in zip(nums, chips):
                cc = lax.rem(c + dc, 2)
                src = sendb.at[n, pl.ds(pl.multiple_of(cc * 32, 32), 32)]
                mine = pl.ds(pl.multiple_of(own * 32, 32), 32)
                if (dz, dy, dc) == (0, 0, 0):
                    recvb[mine, :] = src[...]
                else:
                    cps.append(send(src, recvb.at[mine], ss, rs, first + len(cps), at(dz, dy, dc)))
        return cps

    ld_feat.wait()
    cps_f = []
    for chips in ROUNDS:
        cps_f += halo(chips, F, 0, sendf, recvf, fss, frs, len(cps_f), [])
    for i in range(2):
        pick([1024 + x * B + i * 256 + j * 64 for j in range(4)], 0)
        for t in range(F // 256):
            cols = slice(t * 256, (t + 1) * 256)
            left1[i * 256 : (i + 1) * 256, cols] = dot(sel[...], table[:, cols]).astype(BF)
    ld_hist = load(6, hist_h, table)

    ld_tiles.wait()

    def fill(q, carry):
        rows = pl.ds(pl.multiple_of(q * BLK, BLK), BLK)
        for b in range(NTAB):
            acc = jnp.zeros((BLK, BLK), F32)
            for k in range(KB):
                acc += jnp.where((ids[0, 0, q, k] == b) & (k < counts[0, 0, q]), tiles[q, k], jnp.zeros((), BF)).astype(F32)
            adj[rows, b * BLK : (b + 1) * BLK] = acc.astype(BF)
        return carry

    lax.fori_loop(0, QB, fill, 0)
    adjt[...] = adj[:, :B].T
    ld_hist.wait()
    cps_h = []
    for chips, (k0, k1) in zip(ROUNDS[:3], ((0, 16), (16, 23), (23, 31))):
        cps_h += halo(chips, H, 1, sendh, recvh, hss, hrs, len(cps_h), cps_f[k0:k1])

    ld_w1.wait()
    for t in range(F // 256):
        cols = slice(t * 256, (t + 1) * 256)
        tmp[:, cols] = dot(adj[:, :B], left1[:, cols])
    for t in range(4):
        cols = slice(t * 256, (t + 1) * 256)
        pre1[:, cols] = dot(left1[:, :F], w1[:F, cols])
    for cp in cps_f:
        cp.wait_recv()
    ag = []
    for i in range(2):
        rows = slice(i * 256, (i + 1) * 256)
        left1[rows, F:] = (tmp[rows, :F] + dot(adj[rows, B:], recvf[...])).astype(BF)
        pre = pre1[rows, :] + dot(left1[rows, F:], w1[F:, :])
        sig = jax.nn.sigmoid(pre)
        hid = (pre * sig).astype(BF)
        pre1[rows, :] = swish_slope(pre, sig)
        left2[rows, :H] = hid
        wide = hid.astype(F32)
        scale = (jnp.max(jnp.abs(wide), axis=1, keepdims=True) + 1e-5).astype(BF).astype(F32)
        mine = pl.ds(pl.multiple_of(x * B + i * 256, 256), 256)
        codes[mine, :] = (wide * (1.0 / scale)).astype(BF)
        for j in range(2):
            wide = jnp.broadcast_to(scale[j * 128 : (j + 1) * 128], (128, 128)).T
            scmsg[x, 2 * i + j : 2 * i + j + 1, :] = wide[0:1]
        ag.append(send(codes.at[mine], codes.at[mine], ass, ars, i, at(0, 0, 0, 1)))
    for i in (1, 0):
        mine = pl.ds(pl.multiple_of(x * B + i * 256, 256), 256)
        ag.append(send(codes.at[mine], codes.at[mine], ass, ars, 2 + i, at(0, 0, 0, 3)))
    for dx in (1, 2, 3):
        ag.append(send(scmsg.at[x], scmsg.at[x], ass, ars, 5 + dx, at(0, 0, 0, dx)))

    cps_h += halo(ROUNDS[3], H, 1, sendh, recvh, hss, hrs, len(cps_h), [])

    ld_w2.wait()
    ld_cot.wait()
    for t in range(4):
        cols = slice(t * 256, (t + 1) * 256)
        tmp[:, cols] = dot(adj[:, :B], left2[:, cols])
        pre2[:, cols] = dot(left2[:, :H], w2[:H, cols])
        table[cols, :B] = left2[:, cols].T
    for t in range(6):
        cols = slice(t * 256, (t + 1) * 256)
        table[cols, B:] = left1[:, cols].T

    ag[0].wait_recv()
    far = pl.ds(pl.multiple_of(lax.rem(x + 3, 4) * B, B), 256)
    fwd = [send(codes.at[far], codes.at[far], ass, ars, 4, at(0, 0, 0, 1))]
    ag[2].wait_recv()
    far = pl.ds(pl.multiple_of(lax.rem(x + 1, 4) * B + 256, 256), 256)
    fwd.append(send(codes.at[far], codes.at[far], ass, ars, 5, at(0, 0, 0, 3)))

    for cp in cps_h:
        cp.wait_recv()
    for t in range(4):
        cols = slice(t * 256, (t + 1) * 256)
        agg = (tmp[:, cols] + dot(adj[:, B:], recvh[:, cols])).astype(BF)
        left2[:, H + t * 256 : H + (t + 1) * 256] = agg
        table[H + t * 256 : H + (t + 1) * 256, :B] = agg.T
    for t in range(4):
        cols = slice(t * 256, (t + 1) * 256)
        pre = pre2[:, cols] + dot(left2[:, H:], w2[H:, cols])
        sig = jax.nn.sigmoid(pre)
        d2[:, cols] = (cot[:, cols].astype(F32) * swish_slope(pre, sig)).astype(BF)

    def swap(zt, subs, recv, base):
        return pltpu.make_async_remote_copy(
            src_ref=part.at[zt, :, 1 - c, :, pl.ds(0, subs)], dst_ref=recv.at[zt],
            send_sem=css.at[base], recv_sem=crs.at[base],
            device_id=at(0, 0, 1), device_id_type=MESH,
        )

    def piece(i, lanes, delta, share, recv, base):
        zt = lax.rem(z + i + 1, 4)
        lhs = table[pl.ds(pl.multiple_of(zt * 8 * share, 128), 8 * share), lanes]
        for t in range(4):
            res = dot(lhs, delta[:, t * 256 : (t + 1) * 256]).astype(BF)
            for o in range(8):
                for k in range(share // 8):
                    r0, c0 = o * share + k // 2 * 16, k % 2 * 128
                    part[zt, o // 2, o % 2, t, k] = res[r0 : r0 + 16, c0 : c0 + 128]
        swap(zt, share // 8, recv, base + i).start()

    def merge(i, subs, recv, base):
        zt = lax.rem(z + i + 1, 4)
        swap(zt, subs, recv, base + i).wait()
        for t in range(4):
            both = recv[zt, t].astype(F32) + part[zt, t, c, :, :subs].astype(F32)
            recv[zt, t] = both.astype(BF)

    def wait(cps):
        for cp in cps:
            cp.wait_recv()

    def total(mine, got, *at_index):
        acc = mine.astype(F32)
        for i in range(3):
            acc += got[(i, *at_index)].astype(F32)
        return acc.astype(BF)

    def around(i):
        return [lax.rem(k + i + 1, 4) for k in (z, y, x)]

    cuts2 = ((0, 3), (3, 3), (6, 2))
    cuts1 = ((0, 2), (2, 2), (4, 2))
    bufs2 = (r2, (pa2, pb2, pc2), (qa2, qb2, qc2), (ra2, rb2, rc2), g2, cuts2, 0)
    bufs1 = (r1, (pa1, pb1, pc1), (qa1, qb1, qc1), (ra1, rb1, rc1), g1, cuts1, 48)

    def start_first(i, bufs):
        recv, (pa, pb, pc), _, _, _, cuts, base = bufs
        sa, sb, sc = (pl.ds(*cut) for cut in cuts)
        zt = lax.rem(z + i + 1, 4)
        cps = []
        if i < 3:
            cps.append(send(recv.at[zt, :, :, sb], pb.at[i], rss, rrs, base + i, at(i + 1, 0, 0)))
        for k in range(3):
            _, yy, xx = around(k)
            cps.append(send(recv.at[zt, yy, :, sa], pa.at[k, zt], rss, rrs, base + 3 + 6 * i + k, at(0, k + 1, 0)))
            cps.append(send(recv.at[zt, :, xx, sc], pc.at[k, zt], rss, rrs, base + 6 + 6 * i + k, at(0, 0, 0, k + 1)))
        return cps

    def start_second(bufs):
        recv, (pa, pb, pc), (qa, qb, qc), _, _, cuts, base = bufs
        sa, sb, sc = (slice(a, a + n) for a, n in cuts)

        def one(k, carry):
            recv[k, y, :, sa] = total(recv[k, y, :, sa], pa, k)
            recv[z, k, :, sb] = total(recv[z, k, :, sb], pb, k)
            recv[k, :, x, sc] = total(recv[k, :, x, sc], pc, k)
            return carry

        lax.fori_loop(0, 4, one, 0)
        sa, sb, sc = (pl.ds(*cut) for cut in cuts)
        cps = []
        for i in range(3):
            zz, yy, _ = around(i)
            cps.append(send(recv.at[zz, y, :, sa], qa.at[i], rss, rrs, base + 27 + i, at(i + 1, 0, 0)))
            cps.append(send(recv.at[z, yy, :, sb], qb.at[i], rss, rrs, base + 30 + i, at(0, i + 1, 0)))
            cps.append(send(recv.at[:, yy, x, sc], qc.at[i], rss, rrs, base + 33 + i, at(0, i + 1, 0)))
        return cps

    def start_third(bufs):
        recv, _, (qa, qb, qc), (ra, rb, rc), _, cuts, base = bufs
        sa, sb, sc = (slice(a, a + n) for a, n in cuts)

        def one(k, carry):
            recv[z, y, k, sa] = total(recv[z, y, k, sa], qa, k)
            recv[z, y, k, sb] = total(recv[z, y, k, sb], qb, k)
            recv[k, y, x, sc] = total(recv[k, y, x, sc], qc, k)
            return carry

        lax.fori_loop(0, 4, one, 0)
        sa, sb, sc = (pl.ds(*cut) for cut in cuts)
        cps = []
        for i in range(3):
            zz, _, xx = around(i)
            cps.append(send(recv.at[z, y, xx, sa], ra.at[i], rss, rrs, base + 36 + i, at(0, 0, 0, i + 1)))
            cps.append(send(recv.at[z, y, xx, sb], rb.at[i], rss, rrs, base + 39 + i, at(0, 0, 0, i + 1)))
            cps.append(send(recv.at[zz, y, x, sc], rc.at[i], rss, rrs, base + 42 + i, at(i + 1, 0, 0)))
        return cps

    def start_last(bufs):
        recv, _, _, outs, gath, cuts, base = bufs
        for (a, n), got in zip(cuts, outs):
            gath[x, a : a + n] = total(recv[z, y, x, a : a + n], got)
        return [send(gath.at[x], gath.at[x], rss, rrs, base + 45 + i, at(0, 0, 0, i + 1)) for i in range(3)]

    two = []
    for i in range(4):
        piece(i, slice(0, B), d2, 64, r2, 0)
        if i:
            merge(i - 1, 8, r2, 0)
            two += start_first(i - 1, bufs2)
    for t in range(4):
        cols = slice(t * 256, (t + 1) * 256)
        back = dot_cols(d2[...], w2[H + t * 256 : H + (t + 1) * 256, :]).astype(BF)
        tmp[:, cols] = dot(adjt[...], back)
    merge(3, 8, r2, 0)
    two += start_first(3, bufs2)
    for t in range(4):
        cols = slice(t * 256, (t + 1) * 256)
        grad = tmp[:, cols] + dot_cols(d2[...], w2[cols, :])
        d1[:, cols] = (grad * pre1[:, cols]).astype(BF)
    one = []
    for i in range(4):
        piece(i, slice(B, 2 * B), d1, 48, r1, 4)
        if i:
            merge(i - 1, 6, r1, 4)
            one += start_first(i - 1, bufs1)
    merge(3, 6, r1, 4)
    one += start_first(3, bufs1)

    for cp in [ag[1]] + ag[3:] + fwd:
        cp.wait_recv()
    sub = lax.broadcasted_iota(jnp.int32, (256, 256), 0)

    def place(n, carry):
        for t in range(NODE // 256):
            cols = slice(t * 256, (t + 1) * 256)
            hit = sub + n * 256 == brow[0, t // 2 : t // 2 + 1, t % 2 * 256 : t % 2 * 256 + 256]
            sel[:, cols] = jnp.where(hit, 1.0, 0.0).astype(BF)
        slot = lax.rem(n, 2)
        out = pltpu.make_async_copy(
            stage.at[slot], hist_o.at[pl.ds(pl.multiple_of(n * 256, 256), 256)], osem.at[slot]
        )

        @pl.when(n >= 2)
        def _():
            out.wait()

        for t in range(4):
            cols = slice(t * 256, (t + 1) * 256)
            stage[slot, :, cols] = dot(sel[...], codes[:, cols]).astype(BF)
        out.start()
        return carry

    sc[...] = jnp.zeros((8, NODE), F32)
    lane_w = lax.broadcasted_iota(jnp.int32, (128, 128), 1)

    def place_scale(k, carry):
        rr, j = lax.div(k, 4), lax.rem(k, 4)
        col = idxc[pl.ds(pl.multiple_of(1024 + k * 128, 128), 128), :]
        val = jnp.broadcast_to(scmsg[rr, pl.ds(j, 1), :], (128, 128)).T
        for t in range(NODE // 128):
            got = jnp.where(col == lane_w + t * 128, val, 0.0)
            sc[:, t * 128 : (t + 1) * 128] += jnp.sum(got.reshape(16, 8, 128), axis=0)
        return carry

    wait(two)
    two += start_second(bufs2)
    lax.fori_loop(0, 4, place, 0)
    wait(two[27:])
    two += start_third(bufs2)
    wait(one)
    one += start_second(bufs1)
    lax.fori_loop(4, 7, place, 0)
    wait(two[36:])
    two += start_last(bufs2)
    wait(one[27:])
    one += start_third(bufs1)
    lax.fori_loop(7, 8, place, 0)
    lax.fori_loop(0, 16, place_scale, 0)
    out_sc = load(12, sc, sc_o)
    wait(one[36:])
    one += start_last(bufs1)
    for slot in range(2):
        pltpu.make_async_copy(stage.at[slot], hist_o.at[pl.ds(0, 256)], osem.at[slot]).wait()
    wait(two[45:])
    out_two = load(13, g2, two_o)
    wait(one[45:])
    out_one = load(0, g1, one_o)
    for cp in cps_h + ag + fwd + two + one:
        cp.wait_send()
    for cp in (out_sc, out_two, out_one):
        cp.wait()


def finish(hist_i, sc_i, two_i, one_i, hist_o, sc_o, g1_o, g2_o, room, sc, two, one, line, g1, g2, get, put):
    ins, outs = [], []
    for i in range(8):
        rows = pl.ds(i * 256, 256)
        ins.append(pltpu.make_async_copy(hist_i.at[rows], room.at[i], get.at[i]))
        outs.append(pltpu.make_async_copy(room.at[i], hist_o.at[rows], put.at[i]))
        ins[-1].start()
    small = ((sc_i, sc), (two_i, two), (one_i, one))
    ins_small = [pltpu.make_async_copy(src, dst, get.at[8 + i]) for i, (src, dst) in enumerate(small)]
    for came in ins_small:
        came.start()
    for came, gone in zip(ins, outs):
        came.wait()
        gone.start()
    for came in ins_small:
        came.wait()
    line[...] = jnp.sum(sc[...], axis=0).astype(BF)
    for src, dst, subs in ((two, g2, 8), (one, g1, 6)):
        for t in range(4):
            for k in range(subs):
                r0, c0 = k // 2 * 16, t * 256 + k % 2 * 128
                dst[r0 : r0 + 16, c0 : c0 + 128] = src[t, k].astype(F32)
    for i, (src, dst) in enumerate(((line, sc_o), (g1, g1_o), (g2, g2_o))):
        outs.append(pltpu.make_async_copy(src, dst, put.at[8 + i]))
        outs[-1].start()
    for gone in outs:
        gone.wait()


def shards(feat_codes, feat_scales, hist_codes, hist_scales, batch_rows, send_rows, send_counts,
           block_ids, block_counts, tiles, w_one, w_two, cotangent):
    hbm = pl.BlockSpec(memory_space=pl.ANY)
    smem = pl.BlockSpec(memory_space=pltpu.SMEM)
    v = pltpu.VMEM
    dma = pltpu.SemaphoreType.DMA
    def sums(na, nb, nc):
        tile = (16, 128)
        return [
            v((4, 4, 4, na + nb + nc, *tile), BF),
            v((3, 4, 4, na, *tile), BF), v((3, 4, 4, nb, *tile), BF), v((3, 4, 4, nc, *tile), BF),
            v((3, 4, na, *tile), BF), v((3, 4, nb, *tile), BF), v((3, 4, nc, *tile), BF),
            v((3, na, *tile), BF), v((3, nb, *tile), BF), v((3, nc, *tile), BF),
            v((4, na + nb + nc, *tile), BF),
        ]

    scratch = [
        v((1, 4, B), jnp.int32), v((1, 1, 32, 32), jnp.int32), v((1, 1, 32), jnp.int32), v((NODE,), BF), v((NODE,), BF),
        v((8, NODE), F32),
        v((NODE, H), BF), v((2 * F, H), BF), v((2 * H, H), BF), v((QB, KB, BLK, BLK), BF), v((B, H), BF),
        v((3072, 128), jnp.int32), v((B, NTAB * BLK), BF), v((B, B), BF), v((256, NODE), BF),
        v((16, 64, F), BF), v((16, 64, H), BF), v((1024, F), BF), v((1024, H), BF),
        v((B, 2 * F), BF), v((B, 2 * H), BF), v((B, H), F32), v((B, H), F32), v((B, H), F32),
        v((B, H), BF), v((B, H), BF), v((4 * B, H), BF), v((4, 8, 128), F32), v((2, 256, H), BF),
        v((4, 4, 2, 4, 8, 16, 128), BF), *sums(3, 3, 2), *sums(2, 2, 2),
        dma((14,)), dma((2,)), dma((31,)), dma((31,)), dma((31,)), dma((31,)),
        dma((9,)), dma((9,)), dma((8,)), dma((8,)), dma((96,)), dma((96,)),
    ]
    made = pl.pallas_call(
        kernel,
        out_shape=(
            jax.ShapeDtypeStruct((NODE, H), BF),
            jax.ShapeDtypeStruct((8, NODE), F32),
            jax.ShapeDtypeStruct((4, 8, 16, 128), BF),
            jax.ShapeDtypeStruct((4, 6, 16, 128), BF),
        ),
        in_specs=[smem] * 2 + [hbm] * 11,
        out_specs=(hbm,) * 4,
        scratch_shapes=scratch,
        compiler_params=pltpu.CompilerParams(
            collective_id=0, has_side_effects=True, vmem_limit_bytes=62 << 20
        ),
        cost_estimate=pl.CostEstimate(flops=30_000_000_000, bytes_accessed=30_000_000, transcendentals=1_000_000),
    )(
        block_ids, block_counts, batch_rows, send_rows, send_counts, feat_scales, hist_scales,
        feat_codes, hist_codes, tiles[0, 0], w_one, w_two, cotangent[0, 0],
    )
    return pl.pallas_call(
        finish,
        out_shape=(
            jax.ShapeDtypeStruct((NODE, H), BF),
            jax.ShapeDtypeStruct((NODE,), BF),
            jax.ShapeDtypeStruct((48, H), F32),
            jax.ShapeDtypeStruct((64, H), F32),
        ),
        in_specs=[hbm] * 4,
        out_specs=(hbm,) * 4,
        scratch_shapes=[
            v((8, 256, H), BF), v((8, NODE), F32), v((4, 8, 16, 128), BF), v((4, 6, 16, 128), BF),
            v((NODE,), BF), v((48, H), F32), v((64, H), F32), dma((11,)), dma((11,)),
        ],
        compiler_params=pltpu.CompilerParams(vmem_limit_bytes=60 << 20),
    )(*made)


def solution(mesh):
    in_specs = (
        P("owner", None), P("owner"), P("owner", None), P("owner"), P("owner", None, None),
        P("owner", "rep", None, None), P("owner", "rep", None), P("owner", "rep", None, None),
        P("owner", "rep", None), P("owner", "rep", None, None, None, None), P(), P(),
        P("owner", "rep", None, None),
    )
    out_specs = (P("owner", None), P("owner"), P("owner", None), P("owner", None))
    return jax.shard_map(shards, mesh=mesh, in_specs=in_specs, out_specs=out_specs, check_vma=False)
```

```python
import functools

import jax
import jax.numpy as jnp
from jax import lax
from jax.experimental import pallas as pl
from jax.experimental.pallas import tpu as pltpu
from jax.sharding import PartitionSpec as P

F = 768
H = 1024
B = 512
BLK = 128
KB = 8
QB = 4
NODE = 2048
NTAB = 12
MESH = pl.DeviceIdType.MESH
BF = jnp.bfloat16
F32 = jnp.float32

ROUNDS = (
    ((1, 0), (3, 0), (0, 1), (0, 3)),
    ((1, 1), (3, 3), (1, 3), (3, 1)),
    ((2, 0), (0, 2), (2, 2), (0, 0)),
    ((2, 1), (1, 2), (2, 3), (3, 2)),
)
PEERS = [(dz, dy, dc) for chips in ROUNDS for dc in (0, 1) for dz, dy in chips if (dz, dy, dc) != (0, 0, 0)]


def swish_slope(pre, sig):
    return sig * (1.0 + pre * (1.0 - sig))


def dot(left, right):
    return jnp.dot(left, right, preferred_element_type=F32)


def dot_rows(left, right):
    return lax.dot_general(left, right, (((0,), (0,)), ((), ())), preferred_element_type=F32)


def dot_cols(left, right):
    return lax.dot_general(left, right, (((1,), (1,)), ((), ())), preferred_element_type=F32)


def kernel(
    ids, counts, brow_h, srow_h, scount_h, fscale_h, hscale_h, feat_h, hist_h, tiles_h, w1_h, w2_h, cot_h,
    hist_o, sc_o, two_o, one_o,
    brow, srow, scount, fscale, hscale, sc, scol,
    table, w1, w2, tiles, cot, idxc, adj, adjt, sel, sendf, sendh, recvf, recvh,
    left1, left2, pre1, pre2, tmp, d2, d1, codes, scmsg, stage, part,
    r2, pa2, pb2, pc2, qa2, qb2, qc2, ra2, rb2, rc2, g2,
    r1, pa1, pb1, pc1, qa1, qb1, qc1, ra1, rb1, rc1, g1,
    lsem, osem, fss, frs, hss, hrs, ass, ars, css, crs, rss, rrs,
):
    own = lax.axis_index("owner")
    x = lax.axis_index("rep")
    z = lax.div(own, 8)
    y = lax.rem(lax.div(own, 2), 4)
    c = lax.rem(own, 2)

    def at(dz, dy, dc, dx=0):
        zz, yy = lax.rem(z + dz, 4), lax.rem(y + dy, 4)
        return (zz * 8 + yy * 2 + lax.rem(c + dc, 2), lax.rem(x + dx, 4))

    def load(k, src, dst):
        cp = pltpu.make_async_copy(src, dst, lsem.at[k])
        cp.start()
        return cp

    def send(src, dst, ss, rs, k, dev):
        cp = pltpu.make_async_remote_copy(
            src_ref=src, dst_ref=dst, send_sem=ss.at[k], recv_sem=rs.at[k],
            device_id=dev, device_id_type=MESH,
        )
        cp.start()
        return cp

    bar = pltpu.get_barrier_semaphore()
    for dz, dy, dc in PEERS:
        pl.semaphore_signal(bar, inc=1, device_id=at(dz, dy, dc), device_id_type=MESH)
    for dx in (1, 2, 3):
        pl.semaphore_signal(bar, inc=1, device_id=at(0, 0, 0, dx), device_id_type=MESH)

    smalls = [
        load(7 + i, src, dst)
        for i, (src, dst) in enumerate(
            ((scount_h, scount), (srow_h, srow), (brow_h, brow), (fscale_h, fscale), (hscale_h, hscale))
        )
    ]
    ld_feat = load(1, feat_h, table.at[:, pl.ds(0, F)])
    ld_tiles = load(2, tiles_h, tiles)
    ld_w1 = load(3, w1_h, w1)
    ld_w2 = load(4, w2_h, w2)
    ld_cot = load(5, cot_h, cot)
    for cp in smalls:
        cp.wait()

    alive = lax.broadcasted_iota(jnp.int32, (32, 32), 0) < scount[0]
    turned = jnp.where(alive, srow[0, 0].T, -1)
    for d in range(32):
        idxc[d * 32 : (d + 1) * 32, :] = jnp.broadcast_to(turned[:, d : d + 1], (32, 128))

    line = brow[0, pl.ds(x, 1), :]
    for j in range(4):
        wide = jnp.broadcast_to(line[:, j * 128 : (j + 1) * 128], (128, 128)).T
        idxc[1024 + j * 128 : 1024 + (j + 1) * 128, :] = wide
    scales = (fscale[...].astype(F32).reshape(1, NODE), hscale[...].astype(F32).reshape(1, NODE))

    lane = lax.broadcasted_iota(jnp.int32, (64, 128), 1)

    def pick(starts, which):
        for i, start in enumerate(starts):
            col = idxc[pl.ds(pl.multiple_of(start, 64), 64), :]
            for t in range(NODE // 128):
                hit = col == lane + t * 128
                val = jnp.where(hit, scales[which][:, t * 128 : (t + 1) * 128], 0.0)
                sel[i * 64 : (i + 1) * 64, t * 128 : (t + 1) * 128] = val.astype(BF)

    def halo(chips, width, which, sendb, recvb, ss, rs, first, gate):
        cps = []
        nums = [lax.rem(z + dz, 4) * 4 + lax.rem(y + dy, 4) for dz, dy in chips]
        pick([n * 64 for n in nums], which)
        for t in range(width // 256):
            cols = slice(t * 256, (t + 1) * 256)
            res = dot(sel[...], table[:, cols]).astype(BF)
            for i, n in enumerate(nums):
                sendb[n, :, cols] = res[i * 64 : (i + 1) * 64]
        if first == 0 and width == F:
            pl.semaphore_wait(bar, len(PEERS) + 3)
        for cp in gate:
            cp.wait_send()
        for dc in (0, 1):
            for n, (dz, dy) in zip(nums, chips):
                cc = lax.rem(c + dc, 2)
                src = sendb.at[n, pl.ds(pl.multiple_of(cc * 32, 32), 32)]
                mine = pl.ds(pl.multiple_of(own * 32, 32), 32)
                if (dz, dy, dc) == (0, 0, 0):
                    recvb[mine, :] = src[...]
                else:
                    cps.append(send(src, recvb.at[mine], ss, rs, first + len(cps), at(dz, dy, dc)))
        return cps

    ld_feat.wait()
    cps_f = []
    for chips in ROUNDS:
        cps_f += halo(chips, F, 0, sendf, recvf, fss, frs, len(cps_f), [])
    for i in range(2):
        pick([1024 + i * 256 + j * 64 for j in range(4)], 0)
        for t in range(F // 256):
            cols = slice(t * 256, (t + 1) * 256)
            left1[i * 256 : (i + 1) * 256, cols] = dot(sel[...], table[:, cols]).astype(BF)
    ld_hist = load(6, hist_h, table)

    ld_tiles.wait()

    def fill(q, carry):
        rows = pl.ds(pl.multiple_of(q * BLK, BLK), BLK)
        for b in range(NTAB):
            acc = jnp.zeros((BLK, BLK), F32)
            for k in range(KB):
                acc += jnp.where((ids[0, 0, q, k] == b) & (k < counts[0, 0, q]), tiles[q, k], jnp.zeros((), BF)).astype(F32)
            adj[rows, b * BLK : (b + 1) * BLK] = acc.astype(BF)
        return carry

    lax.fori_loop(0, QB, fill, 0)
    adjt[...] = adj[:, :B].T
    ld_w1.wait()
    for t in range(F // 256):
        cols = slice(t * 256, (t + 1) * 256)
        tmp[:, cols] = dot(adj[:, :B], left1[:, cols])
    for t in range(4):
        cols = slice(t * 256, (t + 1) * 256)
        pre1[:, cols] = dot(left1[:, :F], w1[:F, cols])
    ld_hist.wait()
    cps_h = []
    for chips, (k0, k1) in zip(ROUNDS[:3], ((0, 16), (16, 23), (23, 31))):
        cps_h += halo(chips, H, 1, sendh, recvh, hss, hrs, len(cps_h), cps_f[k0:k1])

    for cp in cps_f:
        cp.wait_recv()
    ag, right, left = [], {}, {}

    def pass_on(q, dx, group, k):
        mine = pl.ds(pl.multiple_of(group * B + q * 128, 128), 128)
        return send(codes.at[mine], codes.at[mine], ass, ars, k, at(0, 0, 0, dx))

    for q in (0, 2, 1, 3):
        rows = slice(q * 128, (q + 1) * 128)
        left1[rows, F:] = (tmp[rows, :F] + dot(adj[rows, B:], recvf[...])).astype(BF)
        pre = pre1[rows, :] + dot(left1[rows, F:], w1[F:, :])
        sig = jax.nn.sigmoid(pre)
        hid = (pre * sig).astype(BF)
        pre1[rows, :] = pre
        left2[rows, :H] = hid
        wide = hid.astype(F32)
        scale = (jnp.max(jnp.abs(wide), axis=1, keepdims=True) + 1e-5).astype(BF).astype(F32)
        codes[pl.ds(pl.multiple_of(x * B + q * 128, 128), 128), :] = (wide * (1.0 / scale)).astype(BF)
        scmsg[x, q : q + 1, :] = jnp.broadcast_to(scale, (128, 128)).T[0:1]
        if q < 2:
            right[q] = pass_on(q, 1, x, q)
        else:
            left[q] = pass_on(q, 3, x, 4 + q)
    for q in (0, 1):
        right[2 + q] = pass_on(2 + q, 1, x, 2 + q)
        left[q] = pass_on(q, 3, x, 4 + q)
    for dx in (1, 2, 3):
        ag.append(send(scmsg.at[x], scmsg.at[x], ass, ars, 11 + dx, at(0, 0, 0, dx)))

    cps_h += halo(ROUNDS[3], H, 1, sendh, recvh, hss, hrs, len(cps_h), [])

    ld_w2.wait()
    ld_cot.wait()
    for t in range(4):
        cols = slice(t * 256, (t + 1) * 256)
        tmp[:, cols] = dot(adj[:, :B], left2[:, cols])
        pre2[:, cols] = dot(left2[:, :H], w2[:H, cols])
        table[cols, :B] = left2[:, cols].T
    for t in range(6):
        cols = slice(t * 256, (t + 1) * 256)
        table[cols, B:] = left1[:, cols].T

    for t in range(4):
        cols = slice(t * 256, (t + 1) * 256)
        pre = pre1[:, cols]
        pre1[:, cols] = swish_slope(pre, jax.nn.sigmoid(pre))

    fwd = []
    for q in (0, 1):
        right[q].wait_recv()
        fwd.append(pass_on(q, 1, lax.rem(x + 3, 4), 8 + q))
    for q in (2, 3):
        left[q].wait_recv()
        fwd.append(pass_on(q, 3, lax.rem(x + 1, 4), 8 + q))

    for cp in cps_h:
        cp.wait_recv()
    for t in range(4):
        cols = slice(t * 256, (t + 1) * 256)
        agg = (tmp[:, cols] + dot(adj[:, B:], recvh[:, cols])).astype(BF)
        left2[:, H + t * 256 : H + (t + 1) * 256] = agg
        table[H + t * 256 : H + (t + 1) * 256, :B] = agg.T
    for t in range(4):
        cols = slice(t * 256, (t + 1) * 256)
        pre = pre2[:, cols] + dot(left2[:, H:], w2[H:, cols])
        sig = jax.nn.sigmoid(pre)
        d2[:, cols] = (cot[:, cols].astype(F32) * swish_slope(pre, sig)).astype(BF)

    def swap(zt, subs, recv, base):
        return pltpu.make_async_remote_copy(
            src_ref=part.at[zt, :, 1 - c, :, pl.ds(0, subs)], dst_ref=recv.at[zt],
            send_sem=css.at[base], recv_sem=crs.at[base],
            device_id=at(0, 0, 1), device_id_type=MESH,
        )

    def piece(i, lanes, delta, share, recv, base):
        zt = lax.rem(z + i + 1, 4)
        lhs = table[pl.ds(pl.multiple_of(zt * 8 * share, 128), 8 * share), lanes]
        for t in range(4):
            res = dot(lhs, delta[:, t * 256 : (t + 1) * 256]).astype(BF)
            for o in range(8):
                for k in range(share // 8):
                    r0, c0 = o * share + k // 2 * 16, k % 2 * 128
                    part[zt, o // 2, o % 2, t, k] = res[r0 : r0 + 16, c0 : c0 + 128]
        swap(zt, share // 8, recv, base + i).start()

    def merge(i, subs, recv, base):
        zt = lax.rem(z + i + 1, 4)
        swap(zt, subs, recv, base + i).wait()
        for t in range(4):
            both = recv[zt, t].astype(F32) + part[zt, t, c, :, :subs].astype(F32)
            recv[zt, t] = both.astype(BF)

    def wait(cps):
        for cp in cps:
            cp.wait_recv()

    def total(mine, got, *at_index):
        acc = mine.astype(F32)
        for i in range(3):
            acc += got[(i, *at_index)].astype(F32)
        return acc.astype(BF)

    def around(i):
        return [lax.rem(k + i + 1, 4) for k in (z, y, x)]

    cuts2 = ((0, 3), (3, 3), (6, 2))
    cuts1 = ((0, 2), (2, 2), (4, 2))
    bufs2 = (r2, (pa2, pb2, pc2), (qa2, qb2, qc2), (ra2, rb2, rc2), g2, cuts2, 0)
    bufs1 = (r1, (pa1, pb1, pc1), (qa1, qb1, qc1), (ra1, rb1, rc1), g1, cuts1, 48)

    def start_first(i, bufs):
        recv, (pa, pb, pc), _, _, _, cuts, base = bufs
        sa, sb, sc = (pl.ds(*cut) for cut in cuts)
        zt = lax.rem(z + i + 1, 4)
        cps = []
        if i < 3:
            cps.append(send(recv.at[zt, :, :, sb], pb.at[i], rss, rrs, base + i, at(i + 1, 0, 0)))
        for k in range(3):
            _, yy, xx = around(k)
            cps.append(send(recv.at[zt, yy, :, sa], pa.at[k, zt], rss, rrs, base + 3 + 6 * i + k, at(0, k + 1, 0)))
            cps.append(send(recv.at[zt, :, xx, sc], pc.at[k, zt], rss, rrs, base + 6 + 6 * i + k, at(0, 0, 0, k + 1)))
        return cps

    def start_second(bufs):
        recv, (pa, pb, pc), (qa, qb, qc), _, _, cuts, base = bufs
        sa, sb, sc = (slice(a, a + n) for a, n in cuts)

        def one(k, carry):
            recv[k, y, :, sa] = total(recv[k, y, :, sa], pa, k)
            recv[z, k, :, sb] = total(recv[z, k, :, sb], pb, k)
            recv[k, :, x, sc] = total(recv[k, :, x, sc], pc, k)
            return carry

        lax.fori_loop(0, 4, one, 0)
        sa, sb, sc = (pl.ds(*cut) for cut in cuts)
        cps = []
        for i in range(3):
            zz, yy, _ = around(i)
            cps.append(send(recv.at[zz, y, :, sa], qa.at[i], rss, rrs, base + 27 + i, at(i + 1, 0, 0)))
            cps.append(send(recv.at[z, yy, :, sb], qb.at[i], rss, rrs, base + 30 + i, at(0, i + 1, 0)))
            cps.append(send(recv.at[:, yy, x, sc], qc.at[i], rss, rrs, base + 33 + i, at(0, i + 1, 0)))
        return cps

    def start_third(bufs):
        recv, _, (qa, qb, qc), (ra, rb, rc), _, cuts, base = bufs
        sa, sb, sc = (slice(a, a + n) for a, n in cuts)

        def one(k, carry):
            recv[z, y, k, sa] = total(recv[z, y, k, sa], qa, k)
            recv[z, y, k, sb] = total(recv[z, y, k, sb], qb, k)
            recv[k, y, x, sc] = total(recv[k, y, x, sc], qc, k)
            return carry

        lax.fori_loop(0, 4, one, 0)
        sa, sb, sc = (pl.ds(*cut) for cut in cuts)
        cps = []
        for i in range(3):
            zz, _, xx = around(i)
            cps.append(send(recv.at[z, y, xx, sa], ra.at[i], rss, rrs, base + 36 + i, at(0, 0, 0, i + 1)))
            cps.append(send(recv.at[z, y, xx, sb], rb.at[i], rss, rrs, base + 39 + i, at(0, 0, 0, i + 1)))
            cps.append(send(recv.at[zz, y, x, sc], rc.at[i], rss, rrs, base + 42 + i, at(i + 1, 0, 0)))
        return cps

    def start_last(bufs):
        recv, _, _, outs, gath, cuts, base = bufs
        for (a, n), got in zip(cuts, outs):
            gath[x, a : a + n] = total(recv[z, y, x, a : a + n], got)
        return [send(gath.at[x], gath.at[x], rss, rrs, base + 45 + i, at(0, 0, 0, i + 1)) for i in range(3)]

    two = []
    for i in range(4):
        piece(i, slice(0, B), d2, 64, r2, 0)
        if i:
            merge(i - 1, 8, r2, 0)
            two += start_first(i - 1, bufs2)
    for t in range(4):
        cols = slice(t * 256, (t + 1) * 256)
        back = dot_cols(d2[...], w2[H + t * 256 : H + (t + 1) * 256, :]).astype(BF)
        tmp[:, cols] = dot(adjt[...], back)
    merge(3, 8, r2, 0)
    two += start_first(3, bufs2)
    for t in range(4):
        cols = slice(t * 256, (t + 1) * 256)
        grad = tmp[:, cols] + dot_cols(d2[...], w2[cols, :])
        d1[:, cols] = (grad * pre1[:, cols]).astype(BF)
    one = []
    for i in range(4):
        piece(i, slice(B, 2 * B), d1, 48, r1, 4)
        if i:
            merge(i - 1, 6, r1, 4)
            one += start_first(i - 1, bufs1)
    merge(3, 6, r1, 4)
    one += start_first(3, bufs1)

    for cp in [right[2], right[3], left[0], left[1]] + ag + fwd:
        cp.wait_recv()
    for k in range(16):
        line = scmsg[k // 4, k % 4 : k % 4 + 1, :]
        scol[k * 128 : (k + 1) * 128, :] = jnp.broadcast_to(line, (128, 128)).T.astype(BF)
    sub = lax.broadcasted_iota(jnp.int32, (256, 256), 0)

    def place(n, carry):
        for t in range(NODE // 256):
            cols = slice(t * 256, (t + 1) * 256)
            hit = sub + n * 256 == brow[0, t // 2 : t // 2 + 1, t % 2 * 256 : t % 2 * 256 + 256]
            sel[:, cols] = jnp.where(hit, 1.0, 0.0).astype(BF)
        slot = lax.rem(n, 2)
        out = pltpu.make_async_copy(
            stage.at[slot], hist_o.at[pl.ds(pl.multiple_of(n * 256, 256), 256)], osem.at[slot]
        )

        @pl.when(n >= 2)
        def _():
            out.wait()

        for t in range(4):
            cols = slice(t * 256, (t + 1) * 256)
            stage[slot, :, cols] = dot(sel[...], codes[:, cols]).astype(BF)
        out.start()
        col = dot(sel[...], scol[...])
        for h in range(2):
            lanes = pl.ds(pl.multiple_of(n * 256 + h * 128, 128), 128)
            sc[:, lanes] = col[h * 128 : (h + 1) * 128].T[:8]
        return carry

    lax.fori_loop(0, 2, place, 0)
    wait(two)
    two += start_second(bufs2)
    lax.fori_loop(2, 4, place, 0)
    wait(two[27:])
    two += start_third(bufs2)
    wait(one)
    one += start_second(bufs1)
    lax.fori_loop(4, 6, place, 0)
    wait(two[36:])
    two += start_last(bufs2)
    wait(one[27:])
    one += start_third(bufs1)
    lax.fori_loop(6, 8, place, 0)
    wait(one[36:])
    one += start_last(bufs1)
    for slot in range(2):
        pltpu.make_async_copy(stage.at[slot], hist_o.at[pl.ds(0, 256)], osem.at[slot]).wait()
    out_sc = load(12, sc, sc_o)
    wait(two[45:])
    out_two = load(13, g2, two_o)
    wait(one[45:])
    out_one = load(0, g1, one_o)
    for cp in cps_h + ag + list(right.values()) + list(left.values()) + fwd + two + one:
        cp.wait_send()
    for cp in (out_sc, out_two, out_one):
        cp.wait()


def finish(hist_i, sc_i, two_i, one_i, hist_o, sc_o, g1_o, g2_o, room, sc, two, one, line, g1, g2, get, put):
    ins, outs = [], []
    for i in range(8):
        rows = pl.ds(i * 256, 256)
        ins.append(pltpu.make_async_copy(hist_i.at[rows], room.at[i], get.at[i]))
        outs.append(pltpu.make_async_copy(room.at[i], hist_o.at[rows], put.at[i]))
        ins[-1].start()
    small = ((sc_i, sc), (two_i, two), (one_i, one))
    ins_small = [pltpu.make_async_copy(src, dst, get.at[8 + i]) for i, (src, dst) in enumerate(small)]
    for came in ins_small:
        came.start()
    for came, gone in zip(ins, outs):
        came.wait()
        gone.start()
    for came in ins_small:
        came.wait()
    line[...] = jnp.max(sc[...], axis=0).astype(BF)
    for src, dst, subs in ((two, g2, 8), (one, g1, 6)):
        for t in range(4):
            for k in range(subs):
                r0, c0 = k // 2 * 16, t * 256 + k % 2 * 128
                dst[r0 : r0 + 16, c0 : c0 + 128] = src[t, k].astype(F32)
    for i, (src, dst) in enumerate(((line, sc_o), (g1, g1_o), (g2, g2_o))):
        outs.append(pltpu.make_async_copy(src, dst, put.at[8 + i]))
        outs[-1].start()
    for gone in outs:
        gone.wait()


def shards(feat_codes, feat_scales, hist_codes, hist_scales, batch_rows, send_rows, send_counts,
           block_ids, block_counts, tiles, w_one, w_two, cotangent):
    hbm = pl.BlockSpec(memory_space=pl.ANY)
    smem = pl.BlockSpec(memory_space=pltpu.SMEM)
    v = pltpu.VMEM
    dma = pltpu.SemaphoreType.DMA
    def sums(na, nb, nc):
        tile = (16, 128)
        return [
            v((4, 4, 4, na + nb + nc, *tile), BF),
            v((3, 4, 4, na, *tile), BF), v((3, 4, 4, nb, *tile), BF), v((3, 4, 4, nc, *tile), BF),
            v((3, 4, na, *tile), BF), v((3, 4, nb, *tile), BF), v((3, 4, nc, *tile), BF),
            v((3, na, *tile), BF), v((3, nb, *tile), BF), v((3, nc, *tile), BF),
            v((4, na + nb + nc, *tile), BF),
        ]

    scratch = [
        v((1, 4, B), jnp.int32), v((1, 1, 32, 32), jnp.int32), v((1, 1, 32), jnp.int32), v((NODE,), BF), v((NODE,), BF),
        v((8, NODE), F32), v((NODE, 128), BF),
        v((NODE, H), BF), v((2 * F, H), BF), v((2 * H, H), BF), v((QB, KB, BLK, BLK), BF), v((B, H), BF),
        v((1536, 128), jnp.int32), v((B, NTAB * BLK), BF), v((B, B), BF), v((256, NODE), BF),
        v((16, 64, F), BF), v((16, 64, H), BF), v((1024, F), BF), v((1024, H), BF),
        v((B, 2 * F), BF), v((B, 2 * H), BF), v((B, H), F32), v((B, H), F32), v((B, H), F32),
        v((B, H), BF), v((B, H), BF), v((4 * B, H), BF), v((4, 8, 128), F32), v((2, 256, H), BF),
        v((4, 4, 2, 4, 8, 16, 128), BF), *sums(3, 3, 2), *sums(2, 2, 2),
        dma((14,)), dma((2,)), dma((31,)), dma((31,)), dma((31,)), dma((31,)),
        dma((15,)), dma((15,)), dma((8,)), dma((8,)), dma((96,)), dma((96,)),
    ]
    made = pl.pallas_call(
        kernel,
        out_shape=(
            jax.ShapeDtypeStruct((NODE, H), BF),
            jax.ShapeDtypeStruct((8, NODE), F32),
            jax.ShapeDtypeStruct((4, 8, 16, 128), BF),
            jax.ShapeDtypeStruct((4, 6, 16, 128), BF),
        ),
        in_specs=[smem] * 2 + [hbm] * 11,
        out_specs=(hbm,) * 4,
        scratch_shapes=scratch,
        compiler_params=pltpu.CompilerParams(
            collective_id=0, has_side_effects=True, vmem_limit_bytes=62 << 20
        ),
        cost_estimate=pl.CostEstimate(flops=30_000_000_000, bytes_accessed=30_000_000, transcendentals=1_000_000),
    )(
        block_ids, block_counts, batch_rows, send_rows, send_counts, feat_scales, hist_scales,
        feat_codes, hist_codes, tiles[0, 0], w_one, w_two, cotangent[0, 0],
    )
    return pl.pallas_call(
        finish,
        out_shape=(
            jax.ShapeDtypeStruct((NODE, H), BF),
            jax.ShapeDtypeStruct((NODE,), BF),
            jax.ShapeDtypeStruct((48, H), F32),
            jax.ShapeDtypeStruct((64, H), F32),
        ),
        in_specs=[hbm] * 4,
        out_specs=(hbm,) * 4,
        scratch_shapes=[
            v((8, 256, H), BF), v((8, NODE), F32), v((4, 8, 16, 128), BF), v((4, 6, 16, 128), BF),
            v((NODE,), BF), v((48, H), F32), v((64, H), F32), dma((11,)), dma((11,)),
        ],
        compiler_params=pltpu.CompilerParams(vmem_limit_bytes=60 << 20),
    )(*made)


def solution(mesh):
    in_specs = (
        P("owner", None), P("owner"), P("owner", None), P("owner"), P("owner", None, None),
        P("owner", "rep", None, None), P("owner", "rep", None), P("owner", "rep", None, None),
        P("owner", "rep", None), P("owner", "rep", None, None, None, None), P(), P(),
        P("owner", "rep", None, None),
    )
    out_specs = (P("owner", None), P("owner"), P("owner", None), P("owner", None))
    return jax.shard_map(shards, mesh=mesh, in_specs=in_specs, out_specs=out_specs, check_vma=False)
```
